512 devices in a mesh: seq: 64 (over z, y), chan: 8 (over x, core).
Axes of the slice: x: 4, y: 4, z: 16, core: 2. Of those that a mesh axis runs over, the one named last changes fastest.
Arguments:
- values: bfloat16 [4096, 8192], P('seq', 'chan'), may hold values from -6 to 6
- gate: bfloat16 [4096, 8192], P('seq', 'chan'), may hold values from -6 to 6
- spectrum: float32 [8192, 2, 8192], P(('chan', 'seq')), may hold values from -6 to 6
- bias: float32 [8192], P('chan'), may hold values from -4 to 4
- out_weight: bfloat16 [8192, 8192], P('chan', 'seq'), may hold values from -0.1875 to 0.1875
Outputs:
- mixed: bfloat16 [4096, 8192], P('seq', 'chan')
The draws below stay inside these ranges and needn't reach their ends.
All inputs are finite; a program needn't handle non-finite values.
Results may differ from the reference program's by a relative error of at most 0.017.
Values may be sent and summed in bfloat16 or wider, within the bound.
No kernel may reach another device: no remote copies, remote signals or barrier semaphores. Data moves between devices by JAX's collectives and lax.ppermute only.
A program may use at most 64 MiB of HBM per device.

```python
import jax
import jax.numpy as jnp
from jax import lax

CHANNELS = 8192
D_OUT = 8192
TOKENS = 4096
FFT_LEN = 8192
N_CHAN = 8


def with_spikes(values, stream_key, source, target, parts, factor):
    owner, partner = [(jnp.arange(values.shape[axis_at]) // (values.shape[axis_at] // parts)).reshape([-1 if axis == axis_at else 1 for axis in range(values.ndim)]) for axis_at in (source, target)]
    chosen = jax.random.permutation(stream_key, parts)[partner]
    strong = (owner == chosen) | (owner == (partner + parts // 2) % parts)
    return jnp.where(strong, factor * values, values)


def block_levels(own_key, dims, cuts, least, high):
    loudness, own = 1.0, jax.random.fold_in(own_key, 6)
    for dim, blocks in cuts:
        steps = jnp.exp(jax.random.uniform(jax.random.fold_in(own, dim), (blocks,), jnp.float32, least / len(cuts), high / len(cuts)))
        loudness = loudness * jnp.repeat(steps, dims[dim] // blocks).reshape([-1 if axis == dim else 1 for axis in range(len(dims))])
    return loudness


def normal_values(stream_key, extent, scale, limit, shards=(), held_as=jnp.bfloat16):
    entries = scale * jax.random.normal(stream_key, extent, jnp.float32)
    if shards:
        entries = entries * block_levels(stream_key, extent, shards, -0.22, 0.18)
    return jnp.clip(entries, -limit, limit).astype(held_as)


def bell_draw_with(stream_key, extent, width, most, shards, heavy, dtype=jnp.bfloat16):
    array = width * jax.random.normal(stream_key, extent, jnp.float32)
    if shards:
        array = array * block_levels(stream_key, extent, shards, -0.22, 0.18)
    return jnp.clip(with_spikes(array, jax.random.fold_in(stream_key, 3), *heavy), -most, most).astype(dtype)


def setup_inputs(seed: int = 0) -> dict:
    arg_keys = jax.random.split(jax.random.key(seed), 6)
    values = normal_values(arg_keys[0], (TOKENS, CHANNELS), 1.0, 6.0, ((0, 64), (1, 8)))
    gate = normal_values(arg_keys[1], (TOKENS, CHANNELS), 1.0, 6.0, ((0, 64), (1, 8)))
    spectrum = normal_values(arg_keys[2], (CHANNELS, 2, FFT_LEN), 1.0, 6.0, ((0, 512),), jnp.float32)
    bias = normal_values(arg_keys[3], (CHANNELS,), 1.0, 4.0, ((0, 8),), jnp.float32)
    out_weight = bell_draw_with(arg_keys[4], (CHANNELS, D_OUT), CHANNELS ** -0.5, 0.1875, ((0, 8), (1, 64)), (0, 1, 64, 4.0))
    return dict(values=values, gate=gate, spectrum=spectrum, bias=bias, out_weight=out_weight)


def conv_block(args):
    signal, filt = args
    length = signal.shape[-1]
    spectral = jnp.fft.fft(signal, n=2 * length, axis=-1)
    product = spectral * (filt[:, 0] + 1j * filt[:, 1])
    result = jnp.real(jnp.fft.ifft(product, axis=-1))[:, :length]
    return result.astype(jnp.bfloat16)


def reference(values, gate, spectrum, bias, out_weight):
    block = 128
    signal = values.astype(jnp.float32).T.reshape(CHANNELS // block, block, TOKENS)
    filt = spectrum.reshape(CHANNELS // block, block, 2, FFT_LEN)
    conv = lax.map(conv_block, (signal, filt)).reshape(CHANNELS, TOKENS).T
    gated = (gate.astype(jnp.float32) * (conv.astype(jnp.float32) + bias[None, :] * values.astype(jnp.float32))).astype(jnp.bfloat16)
    group = CHANNELS // N_CHAN
    total = jnp.zeros((TOKENS, D_OUT), jnp.float32)
    for index in range(N_CHAN):
        piece = jnp.dot(gated[:, index * group:(index + 1) * group], out_weight[index * group:(index + 1) * group], preferred_element_type=jnp.float32)
        total = total + piece.astype(jnp.bfloat16).astype(jnp.float32)
    return total.astype(jnp.bfloat16)
```

```python
import jax
import jax.numpy as jnp
import numpy as np
from jax import lax
from jax.experimental import pallas as pl
from jax.experimental.pallas import tpu as pltpu
from jax.sharding import Mesh, PartitionSpec as P

Z, Y, X, CORE = 16, 4, 4, 2
HALF = 64
TALL = 128
FFT = 8192


def split(table):
    top = table.astype(jnp.bfloat16)
    rest = (table - top.astype(np.float64)).astype(jnp.bfloat16)
    return top, rest


def fft_tables():
    turn = 2.0 * np.pi
    k, s, m = np.arange(TALL), np.arange(HALF), np.arange(HALF)
    one = turn * (np.outer(k, s) % TALL) / TALL
    first = np.concatenate([np.cos(one), np.sin(one)], 0)
    first = np.concatenate(split(first), 1)
    spin = turn * np.outer(k, m) / FFT
    cos, sin = np.cos(spin), np.sin(spin)
    fwd = np.stack([np.concatenate([cos, -sin], 1), np.concatenate([-sin, -cos], 1)])
    inv = np.stack([np.concatenate([cos, cos], 1), np.concatenate([-sin, sin], 1)])
    two = turn * (np.outer(m, m) % HALF) / HALF
    c2, s2 = np.cos(two), np.sin(two)
    ahead = np.block([[c2, -s2, -s2, c2], [s2, c2, c2, s2]])
    back = np.block([[c2, s2, s2, c2], [-s2, c2, c2, -s2]])

    def triple(table):
        top, rest = split(table)
        return np.concatenate([top, top, rest], 0)

    four = turn * (np.outer(s, k) % TALL) / TALL
    last = np.concatenate([np.cos(four), -np.sin(four)], 0) / FFT
    top, rest = split(last)
    last = np.concatenate([top, top, rest], 1)
    return (
        first,
        np.concatenate([fwd, inv]).astype(np.float32),
        np.stack([triple(ahead), triple(back)]),
        last,
    )


def pieces(value):
    top = value.astype(jnp.bfloat16)
    rest = (value - top.astype(jnp.float32)).astype(jnp.bfloat16)
    return [top, rest, top]


def conv_kernel(sig_ref, spec_ref, first_ref, spin_ref, mid_ref, last_ref, out_ref):
    width = 2 * HALF
    left = lax.broadcasted_iota(jnp.int32, (1, width), 1) < HALF
    fp, fq, ip, iq = [spin_ref[i] for i in range(4)]

    def swap(value):
        return pltpu.roll(value, HALF, 1)

    def dot(one, two):
        return jnp.dot(one, two, preferred_element_type=jnp.float32)

    for pair in range(sig_ref.shape[1] // width):
        lanes = slice(pair * width, (pair + 1) * width)
        data = sig_ref[:, lanes].astype(jnp.float32)
        other = swap(data)
        wide = jnp.concatenate([jnp.where(left, data, other), jnp.where(left, other, data)], 1)
        wide = wide.astype(jnp.bfloat16)
        both = dot(first_ref[...], jnp.concatenate([wide, wide], 0))
        turned = jnp.concatenate(
            [
                both[:TALL, c * width : (c + 1) * width] * fp + both[TALL:, c * width : (c + 1) * width] * fq
                for c in range(2)
            ],
            0,
        )
        freq = dot(jnp.concatenate(pieces(turned), 1), mid_ref[0])
        filt = jnp.concatenate([spec_ref[2 * pair + c].T for c in range(2)], 0)
        turned_filt = swap(filt)
        prod = freq[:, :width] * jnp.where(left, filt, turned_filt) + freq[:, width:] * jnp.where(
            left, -turned_filt, filt
        )
        back = dot(jnp.concatenate(pieces(prod), 1), mid_ref[1])
        spun = jnp.concatenate(
            [
                back[c * TALL : (c + 1) * TALL, :width] * ip + back[c * TALL : (c + 1) * TALL, width:] * iq
                for c in range(2)
            ],
            1,
        )
        ends = dot(last_ref[...], jnp.concatenate(pieces(spun), 0))
        even, odd = ends[:, :width], ends[:, width:]
        conv = jnp.where(left, even[:HALF], odd[HALF:]) + swap(jnp.where(left, odd[:HALF], even[HALF:]))
        out_ref[:, lanes] = conv.astype(jnp.bfloat16)


def long_conv(sig, spec):
    tables = fft_tables()
    vmem = pl.BlockSpec(memory_space=pltpu.VMEM)
    return pl.pallas_call(
        conv_kernel,
        out_shape=jax.ShapeDtypeStruct(sig.shape, jnp.bfloat16),
        in_specs=[vmem] * 6,
        out_specs=vmem,
        compiler_params=pltpu.CompilerParams(vmem_limit_bytes=32 * 1024 * 1024),
        cost_estimate=pl.CostEstimate(flops=1_200_000_000, bytes_accessed=2_000_000, transcendentals=0),
        name="long_conv",
    )(sig, spec, *[jnp.asarray(t) for t in tables])


def turn_kernel(left_ref, out_ref):
    near, far = left_ref.shape[:2]
    blocks = [left_ref[a, b] for b in range(far) for a in range(near)]
    out_ref[...] = jnp.concatenate(blocks, 0).T


def turn(left):
    near, far, width, tokens = left.shape
    vmem = pl.BlockSpec(memory_space=pltpu.VMEM)
    return pl.pallas_call(
        turn_kernel,
        out_shape=jax.ShapeDtypeStruct((tokens, near * far * width), jnp.bfloat16),
        in_specs=[vmem],
        out_specs=vmem,
        compiler_params=pltpu.CompilerParams(vmem_limit_bytes=16 * 1024 * 1024),
        name="turn",
    )(left)


def project_kernel(left_ref, weight_ref, out_ref, held_ref, sems):
    blocks, _, cols = weight_ref.shape
    copies = [pltpu.make_async_copy(weight_ref.at[i], held_ref.at[i], sems.at[i]) for i in range(blocks)]
    for copy in copies:
        copy.start()
    left = left_ref[...]
    step = blocks // (X * CORE)
    for i in range(X * CORE):
        for p in range(step):
            copies[i * step + p].wait()
        weight = jnp.concatenate([held_ref[i * step + p] for p in range(step)], 1)
        part = jnp.dot(left, weight, preferred_element_type=jnp.float32).astype(jnp.bfloat16)
        out_ref[i % CORE, :, i // CORE] = part.reshape(out_ref.shape[1], HALF, step * cols)


def project(left, weight):
    tokens, depth = left.shape
    blocks, _, cols = weight.shape
    wide = blocks // (X * CORE) * cols
    vmem = pl.BlockSpec(memory_space=pltpu.VMEM)
    return pl.pallas_call(
        project_kernel,
        out_shape=jax.ShapeDtypeStruct((CORE, tokens // HALF, X, HALF, wide), jnp.bfloat16),
        in_specs=[vmem, pl.BlockSpec(memory_space=pl.ANY)],
        out_specs=vmem,
        scratch_shapes=[pltpu.VMEM(weight.shape, weight.dtype), pltpu.SemaphoreType.DMA((blocks,))],
        compiler_params=pltpu.CompilerParams(vmem_limit_bytes=52 * 1024 * 1024),
        cost_estimate=pl.CostEstimate(flops=2 * depth * tokens * blocks * cols, bytes_accessed=6_000_000, transcendentals=0),
        name="project",
    )(left, weight)


def gather_kernel(part_ref, out_ref):
    cols = out_ref.shape[1] // (part_ref.shape[0] * 2)
    for y in range(part_ref.shape[0]):
        total = part_ref[y, 0].astype(jnp.float32)
        for x in range(1, part_ref.shape[1]):
            total = total + part_ref[y, x].astype(jnp.float32)
        total = total.astype(jnp.bfloat16)
        for p in range(2):
            at = (p * part_ref.shape[0] + y) * cols
            out_ref[:, at : at + cols] = total[:, p * cols : (p + 1) * cols]


def gather(part):
    vmem = pl.BlockSpec(memory_space=pltpu.VMEM)
    return pl.pallas_call(
        gather_kernel,
        out_shape=jax.ShapeDtypeStruct((part.shape[2], part.shape[0] * part.shape[3]), jnp.bfloat16),
        in_specs=[vmem],
        out_specs=vmem,
        compiler_params=pltpu.CompilerParams(vmem_limit_bytes=16 * 1024 * 1024),
        name="gather",
    )(part)


def per_device(values, gate, spectrum, bias, out_weight):
    rows, group = values.shape
    width = group // (Z * Y)
    cols = out_weight.shape[1]
    weight = lax.all_gather(out_weight, "z", axis=0, tiled=False)

    def by_y(array):
        return array.T.reshape(Z, Y, width, rows).transpose(1, 0, 2, 3).reshape(Y, Z, width * rows)

    near = jnp.concatenate([by_y(values), by_y(gate)], axis=1)
    near = lax.all_to_all(near, "y", split_axis=0, concat_axis=0, tiled=True)
    sig, gat = near[:, :Z], near[:, Z:]
    moved = lax.all_to_all(sig.transpose(1, 0, 2), "z", split_axis=0, concat_axis=0, tiled=True)
    conv = long_conv(moved.reshape(Z * Y, width * rows), spectrum.reshape(width, TALL, TALL))
    conv = lax.all_to_all(conv.reshape(Z, Y, width * rows), "z", split_axis=0, concat_axis=0, tiled=True)
    skip = lax.dynamic_index_in_dim(bias.reshape(Z, Y, width), lax.axis_index("y"), 1, keepdims=False)
    skip = jnp.broadcast_to(skip[:, :, None], (Z, width, rows)).reshape(Z, width * rows)
    conv = conv.transpose(1, 0, 2).astype(jnp.float32)
    gated = (gat.astype(jnp.float32) * (conv + skip[None] * sig.astype(jnp.float32))).astype(jnp.bfloat16)

    left = gated.reshape(Y, Z, width, rows).transpose(1, 2, 0, 3).reshape(Z, width, Y * rows)
    wide = jnp.broadcast_to(left[None], (Y,) + left.shape)
    wide = lax.all_to_all(wide, "y", split_axis=0, concat_axis=0, tiled=True)

    part = project(turn(wide), weight)
    part = lax.all_to_all(part, "core", split_axis=0, concat_axis=0, tiled=True)
    part = (part[0].astype(jnp.float32) + part[1].astype(jnp.float32)).astype(jnp.bfloat16)
    part = part.reshape((Y * X,) + part.shape[2:])
    part = lax.all_to_all(part, ("y", "x"), split_axis=0, concat_axis=0, tiled=True)
    return gather(part.reshape(Y, X, rows, -1))


def solution(mesh):
    names = ("z", "y", "x", "core")
    fine = Mesh(mesh.devices.reshape(Z, Y, X, CORE), names)
    seq, chan = names[:2], names[2:]
    placed = (
        P(seq, chan),
        P(seq, chan),
        P(chan + seq, None, None),
        P(chan),
        P(chan, seq),
    )
    return jax.shard_map(
        per_device, mesh=fine, in_specs=placed, out_specs=P(seq, chan), check_vma=False
    )
```

```python
import jax
import jax.numpy as jnp
import numpy as np
from jax import lax
from jax.experimental import pallas as pl
from jax.experimental.pallas import tpu as pltpu
from jax.sharding import Mesh, PartitionSpec as P

Z, Y, X, CORE = 16, 4, 4, 2
HALF = 64
TALL = 128
FFT = 8192


def split(table):
    top = table.astype(jnp.bfloat16)
    rest = (table - top.astype(np.float64)).astype(jnp.bfloat16)
    return top, rest


def fft_tables():
    turn = 2.0 * np.pi
    k, s, m = np.arange(TALL), np.arange(HALF), np.arange(HALF)
    one = turn * (np.outer(k, s) % TALL) / TALL
    first = np.concatenate([np.cos(one), np.sin(one)], 0)
    first = np.concatenate(split(first), 1)
    spin = turn * np.outer(k, m) / FFT
    cos, sin = np.cos(spin), np.sin(spin)
    fwd = np.stack([np.concatenate([cos, -sin], 1), np.concatenate([-sin, -cos], 1)])
    inv = np.stack([np.concatenate([cos, cos], 1), np.concatenate([-sin, sin], 1)])
    two = turn * (np.outer(m, m) % HALF) / HALF
    c2, s2 = np.cos(two), np.sin(two)
    ahead = np.block([[c2, -s2, -s2, c2], [s2, c2, c2, s2]])
    back = np.block([[c2, s2, s2, c2], [-s2, c2, c2, -s2]])

    def triple(table):
        top, rest = split(table)
        return np.concatenate([top, top, rest], 0)

    four = turn * (np.outer(s, k) % TALL) / TALL
    last = np.concatenate([np.cos(four), -np.sin(four)], 0) / FFT
    top, rest = split(last)
    last = np.concatenate([top, top, rest], 1)
    return (
        first,
        np.concatenate([fwd, inv]).astype(np.float32),
        np.stack([triple(ahead), triple(back)]),
        last,
    )


def pieces(value):
    top = value.astype(jnp.bfloat16)
    rest = (value - top.astype(jnp.float32)).astype(jnp.bfloat16)
    return [top, rest, top]


def conv_kernel(sig_ref, spec_ref, first_ref, spin_ref, mid_ref, last_ref, out_ref):
    width = 2 * HALF
    left = lax.broadcasted_iota(jnp.int32, (1, width), 1) < HALF
    fp, fq, ip, iq = [spin_ref[i] for i in range(4)]

    def swap(value):
        return pltpu.roll(value, HALF, 1)

    def dot(one, two):
        return jnp.dot(one, two, preferred_element_type=jnp.float32)

    for pair in range(sig_ref.shape[1] // width):
        lanes = slice(pair * width, (pair + 1) * width)
        data = sig_ref[:, lanes].astype(jnp.float32)
        other = swap(data)
        wide = jnp.concatenate([jnp.where(left, data, other), jnp.where(left, other, data)], 1)
        wide = wide.astype(jnp.bfloat16)
        both = dot(first_ref[...], jnp.concatenate([wide, wide], 0))
        turned = jnp.concatenate(
            [
                both[:TALL, c * width : (c + 1) * width] * fp + both[TALL:, c * width : (c + 1) * width] * fq
                for c in range(2)
            ],
            0,
        )
        freq = dot(jnp.concatenate(pieces(turned), 1), mid_ref[0])
        filt = jnp.concatenate([spec_ref[2 * pair + c].T for c in range(2)], 0)
        turned_filt = swap(filt)
        prod = freq[:, :width] * jnp.where(left, filt, turned_filt) + freq[:, width:] * jnp.where(
            left, -turned_filt, filt
        )
        back = dot(jnp.concatenate(pieces(prod), 1), mid_ref[1])
        spun = jnp.concatenate(
            [
                back[c * TALL : (c + 1) * TALL, :width] * ip + back[c * TALL : (c + 1) * TALL, width:] * iq
                for c in range(2)
            ],
            1,
        )
        ends = dot(last_ref[...], jnp.concatenate(pieces(spun), 0))
        even, odd = ends[:, :width], ends[:, width:]
        conv = jnp.where(left, even[:HALF], odd[HALF:]) + swap(jnp.where(left, odd[:HALF], even[HALF:]))
        out_ref[:, lanes] = conv.astype(jnp.bfloat16)


def long_conv(sig, spec):
    tables = fft_tables()
    vmem = pl.BlockSpec(memory_space=pltpu.VMEM)
    return pl.pallas_call(
        conv_kernel,
        out_shape=jax.ShapeDtypeStruct(sig.shape, jnp.bfloat16),
        in_specs=[vmem] * 6,
        out_specs=vmem,
        compiler_params=pltpu.CompilerParams(vmem_limit_bytes=32 * 1024 * 1024),
        cost_estimate=pl.CostEstimate(flops=1_200_000_000, bytes_accessed=2_000_000, transcendentals=0),
        name="long_conv",
    )(sig, spec, *[jnp.asarray(t) for t in tables])


def turn_kernel(left_ref, out_ref):
    near, far = left_ref.shape[:2]
    blocks = [left_ref[a, b] for b in range(far) for a in range(near)]
    out_ref[...] = jnp.concatenate(blocks, 0).T


def turn(left):
    near, far, width, tokens = left.shape
    vmem = pl.BlockSpec(memory_space=pltpu.VMEM)
    return pl.pallas_call(
        turn_kernel,
        out_shape=jax.ShapeDtypeStruct((tokens, near * far * width), jnp.bfloat16),
        in_specs=[vmem],
        out_specs=vmem,
        compiler_params=pltpu.CompilerParams(vmem_limit_bytes=16 * 1024 * 1024),
        name="turn",
    )(left)


def project_kernel(me_ref, left_ref, weight_ref, keep_ref, send_ref, held_ref, sems):
    blocks, _, cols = weight_ref.shape
    copies = [pltpu.make_async_copy(weight_ref.at[i], held_ref.at[i], sems.at[i]) for i in range(blocks)]
    for copy in copies:
        copy.start()
    left = left_ref[...]
    step = blocks // X
    pair = step // CORE
    mine = me_ref[0]
    for x in range(X):
        for p in range(step):
            copies[x * step + p].wait()
        order = [x * step + core * pair + p for core in (mine, 1 - mine) for p in range(pair)]
        weight = jnp.concatenate([held_ref[i] for i in order], 1)
        part = jnp.dot(left, weight, preferred_element_type=jnp.float32).astype(jnp.bfloat16)
        keep_ref[:, x] = part[:, : pair * cols].reshape(keep_ref.shape[0], HALF, pair * cols)
        send_ref[:, x] = part[:, pair * cols :].reshape(keep_ref.shape[0], HALF, pair * cols)


def project(me, left, weight):
    tokens, depth = left.shape
    blocks, _, cols = weight.shape
    wide = blocks // (X * CORE) * cols
    vmem = pl.BlockSpec(memory_space=pltpu.VMEM)
    return pl.pallas_call(
        project_kernel,
        out_shape=[jax.ShapeDtypeStruct((tokens // HALF, X, HALF, wide), jnp.bfloat16)] * 2,
        in_specs=[pl.BlockSpec(memory_space=pltpu.SMEM), vmem, pl.BlockSpec(memory_space=pl.ANY)],
        out_specs=[vmem, vmem],
        scratch_shapes=[pltpu.VMEM(weight.shape, weight.dtype), pltpu.SemaphoreType.DMA((blocks,))],
        compiler_params=pltpu.CompilerParams(vmem_limit_bytes=52 * 1024 * 1024),
        cost_estimate=pl.CostEstimate(flops=2 * depth * tokens * blocks * cols, bytes_accessed=6_000_000, transcendentals=0),
        name="project",
    )(me, left, weight)


def gather_kernel(part_ref, out_ref):
    cols = out_ref.shape[1] // (part_ref.shape[0] * 2)
    for y in range(part_ref.shape[0]):
        total = part_ref[y, 0].astype(jnp.float32)
        for x in range(1, part_ref.shape[1]):
            total = total + part_ref[y, x].astype(jnp.float32)
        total = total.astype(jnp.bfloat16)
        for p in range(2):
            at = (p * part_ref.shape[0] + y) * cols
            out_ref[:, at : at + cols] = total[:, p * cols : (p + 1) * cols]


def gather(part):
    vmem = pl.BlockSpec(memory_space=pltpu.VMEM)
    return pl.pallas_call(
        gather_kernel,
        out_shape=jax.ShapeDtypeStruct((part.shape[2], part.shape[0] * part.shape[3]), jnp.bfloat16),
        in_specs=[vmem],
        out_specs=vmem,
        compiler_params=pltpu.CompilerParams(vmem_limit_bytes=16 * 1024 * 1024),
        name="gather",
    )(part)


def per_device(values, gate, spectrum, bias, out_weight):
    rows, group = values.shape
    width = group // (Z * Y)
    cols = out_weight.shape[1]
    weight = lax.all_gather(out_weight, "z", axis=0, tiled=False)

    def by_y(array):
        return array.T.reshape(Z, Y, width, rows).transpose(1, 0, 2, 3).reshape(Y, Z, width * rows)

    near = jnp.concatenate([by_y(values), by_y(gate)], axis=1)
    near = lax.all_to_all(near, "y", split_axis=0, concat_axis=0, tiled=True)
    sig, gat = near[:, :Z], near[:, Z:]
    moved = lax.all_to_all(sig.transpose(1, 0, 2), "z", split_axis=0, concat_axis=0, tiled=True)
    conv = long_conv(moved.reshape(Z * Y, width * rows), spectrum.reshape(width, TALL, TALL))
    conv = lax.all_to_all(conv.reshape(Z, Y, width * rows), "z", split_axis=0, concat_axis=0, tiled=True)
    skip = lax.dynamic_index_in_dim(bias.reshape(Z, Y, width), lax.axis_index("y"), 1, keepdims=False)
    skip = jnp.broadcast_to(skip[:, :, None], (Z, width, rows)).reshape(Z, width * rows)
    conv = conv.transpose(1, 0, 2).astype(jnp.float32)
    gated = (gat.astype(jnp.float32) * (conv + skip[None] * sig.astype(jnp.float32))).astype(jnp.bfloat16)

    left = gated.reshape(Y, Z, width, rows).transpose(1, 2, 0, 3).reshape(Z, width, Y * rows)
    wide = jnp.broadcast_to(left[None], (Y,) + left.shape)
    wide = lax.all_to_all(wide, "y", split_axis=0, concat_axis=0, tiled=True)

    me = lax.axis_index("core").astype(jnp.int32).reshape(1)
    keep, send = project(me, turn(wide), weight)
    other = lax.ppermute(send, "core", [(0, 1), (1, 0)])
    part = (keep.astype(jnp.float32) + other.astype(jnp.float32)).astype(jnp.bfloat16)
    part = part.reshape((Y * X,) + part.shape[2:])
    part = lax.all_to_all(part, ("y", "x"), split_axis=0, concat_axis=0, tiled=True)
    return gather(part.reshape(Y, X, rows, -1))


def solution(mesh):
    names = ("z", "y", "x", "core")
    fine = Mesh(mesh.devices.reshape(Z, Y, X, CORE), names)
    seq, chan = names[:2], names[2:]
    placed = (
        P(seq, chan),
        P(seq, chan),
        P(chan + seq, None, None),
        P(chan),
        P(chan, seq),
    )
    return jax.shard_map(
        per_device, mesh=fine, in_specs=placed, out_specs=P(seq, chan), check_vma=False
    )
```

```python
import jax
import jax.numpy as jnp
import numpy as np
from jax import lax
from jax.experimental import pallas as pl
from jax.experimental.pallas import tpu as pltpu
from jax.sharding import Mesh, PartitionSpec as P

Z, Y, X, CORE = 16, 4, 4, 2
HALF = 64
TALL = 128
FFT = 8192


def split(table):
    top = table.astype(jnp.bfloat16)
    rest = (table - top.astype(np.float64)).astype(jnp.bfloat16)
    return top, rest


def fft_tables():
    turn = 2.0 * np.pi
    k, s, m = np.arange(TALL), np.arange(HALF), np.arange(HALF)
    one = turn * (np.outer(k, s) % TALL) / TALL
    first = np.concatenate([np.cos(one), np.sin(one)], 0)
    first = np.concatenate(split(first), 1)
    spin = turn * np.outer(k, m) / FFT
    cos, sin = np.cos(spin), np.sin(spin)
    fwd = np.stack([np.concatenate([cos, -sin], 1), np.concatenate([-sin, -cos], 1)])
    inv = np.stack([np.concatenate([cos, cos], 1), np.concatenate([-sin, sin], 1)])
    two = turn * (np.outer(m, m) % HALF) / HALF
    c2, s2 = np.cos(two), np.sin(two)
    ahead = np.block([[c2, -s2, -s2, c2], [s2, c2, c2, s2]])
    back = np.block([[c2, s2, s2, c2], [-s2, c2, c2, -s2]])

    def triple(table):
        top, rest = split(table)
        return np.concatenate([top, top, rest], 0)

    four = turn * (np.outer(s, k) % TALL) / TALL
    last = np.concatenate([np.cos(four), -np.sin(four)], 0) / FFT
    top, rest = split(last)
    last = np.concatenate([top, top, rest], 1)
    return (
        first,
        np.concatenate([fwd, inv]).astype(np.float32),
        np.stack([triple(ahead), triple(back)]),
        last,
    )


def pieces(value):
    top = value.astype(jnp.bfloat16)
    rest = (value - top.astype(jnp.float32)).astype(jnp.bfloat16)
    return [top, rest, top]


def conv_kernel(sig_ref, spec_ref, first_ref, spin_ref, mid_ref, last_ref, out_ref):
    width = 2 * HALF
    left = lax.broadcasted_iota(jnp.int32, (1, width), 1) < HALF
    fp, fq, ip, iq = [spin_ref[i] for i in range(4)]

    def swap(value):
        return pltpu.roll(value, HALF, 1)

    def dot(one, two):
        return jnp.dot(one, two, preferred_element_type=jnp.float32)

    for pair in range(sig_ref.shape[1] // width):
        lanes = slice(pair * width, (pair + 1) * width)
        data = sig_ref[:, lanes].astype(jnp.float32)
        other = swap(data)
        wide = jnp.concatenate([jnp.where(left, data, other), jnp.where(left, other, data)], 1)
        wide = wide.astype(jnp.bfloat16)
        both = dot(first_ref[...], jnp.concatenate([wide, wide], 0))
        turned = jnp.concatenate(
            [
                both[:TALL, c * width : (c + 1) * width] * fp + both[TALL:, c * width : (c + 1) * width] * fq
                for c in range(2)
            ],
            0,
        )
        freq = dot(jnp.concatenate(pieces(turned), 1), mid_ref[0])
        filt = jnp.concatenate([spec_ref[2 * pair + c].T for c in range(2)], 0)
        turned_filt = swap(filt)
        prod = freq[:, :width] * jnp.where(left, filt, turned_filt) + freq[:, width:] * jnp.where(
            left, -turned_filt, filt
        )
        back = dot(jnp.concatenate(pieces(prod), 1), mid_ref[1])
        spun = jnp.concatenate(
            [
                back[c * TALL : (c + 1) * TALL, :width] * ip + back[c * TALL : (c + 1) * TALL, width:] * iq
                for c in range(2)
            ],
            1,
        )
        ends = dot(last_ref[...], jnp.concatenate(pieces(spun), 0))
        even, odd = ends[:, :width], ends[:, width:]
        conv = jnp.where(left, even[:HALF], odd[HALF:]) + swap(jnp.where(left, odd[:HALF], even[HALF:]))
        out_ref[:, lanes] = conv.astype(jnp.bfloat16)


def long_conv(sig, spec):
    tables = fft_tables()
    vmem = pl.BlockSpec(memory_space=pltpu.VMEM)
    return pl.pallas_call(
        conv_kernel,
        out_shape=jax.ShapeDtypeStruct(sig.shape, jnp.bfloat16),
        in_specs=[vmem] * 6,
        out_specs=vmem,
        compiler_params=pltpu.CompilerParams(vmem_limit_bytes=32 * 1024 * 1024),
        cost_estimate=pl.CostEstimate(flops=1_200_000_000, bytes_accessed=2_000_000, transcendentals=0),
        name="long_conv",
    )(sig, spec, *[jnp.asarray(t) for t in tables])


def turn_kernel(left_ref, out_ref):
    near, far = left_ref.shape[:2]
    blocks = [left_ref[a, b] for b in range(far) for a in range(near)]
    out_ref[...] = jnp.concatenate(blocks, 0).T


def turn(left):
    near, far, width, tokens = left.shape
    vmem = pl.BlockSpec(memory_space=pltpu.VMEM)
    return pl.pallas_call(
        turn_kernel,
        out_shape=jax.ShapeDtypeStruct((tokens, near * far * width), jnp.bfloat16),
        in_specs=[vmem],
        out_specs=vmem,
        compiler_params=pltpu.CompilerParams(vmem_limit_bytes=16 * 1024 * 1024),
        name="turn",
    )(left)


def project_kernel(side_ref, left_ref, weight_ref, out_ref, held_ref, sems):
    blocks, _, cols = held_ref.shape
    pair = blocks // X
    source = [(x * CORE + side_ref[0]) * pair + p for x in range(X) for p in range(pair)]
    copies = [pltpu.make_async_copy(weight_ref.at[source[i]], held_ref.at[i], sems.at[i]) for i in range(blocks)]
    for copy in copies:
        copy.start()
    left = left_ref[...]
    for x in range(0, X, 2):
        for i in range(x * pair, (x + 2) * pair):
            copies[i].wait()
        weight = jnp.concatenate([held_ref[i] for i in range(x * pair, (x + 2) * pair)], 1)
        part = jnp.dot(left, weight, preferred_element_type=jnp.float32).astype(jnp.bfloat16)
        for k in range(2):
            piece = part[:, k * pair * cols : (k + 1) * pair * cols]
            out_ref[:, x + k] = piece.reshape(out_ref.shape[0], HALF, pair * cols)


def project(side, left, weight, name):
    tokens, depth = left.shape
    blocks, _, cols = weight.shape
    half = blocks // CORE
    wide = half // X * cols
    vmem = pl.BlockSpec(memory_space=pltpu.VMEM)
    return pl.pallas_call(
        project_kernel,
        out_shape=jax.ShapeDtypeStruct((tokens // HALF, X, HALF, wide), jnp.bfloat16),
        in_specs=[pl.BlockSpec(memory_space=pltpu.SMEM), vmem, pl.BlockSpec(memory_space=pl.ANY)],
        out_specs=vmem,
        scratch_shapes=[pltpu.VMEM((half, depth, cols), weight.dtype), pltpu.SemaphoreType.DMA((half,))],
        compiler_params=pltpu.CompilerParams(vmem_limit_bytes=52 * 1024 * 1024),
        cost_estimate=pl.CostEstimate(flops=2 * depth * tokens * half * cols, bytes_accessed=3_000_000, transcendentals=0),
        name=name,
    )(side, left, weight)


def gather_kernel(part_ref, out_ref):
    cols = out_ref.shape[1] // (part_ref.shape[0] * 2)
    for y in range(part_ref.shape[0]):
        total = part_ref[y, 0].astype(jnp.float32)
        for x in range(1, part_ref.shape[1]):
            total = total + part_ref[y, x].astype(jnp.float32)
        total = total.astype(jnp.bfloat16)
        for p in range(2):
            at = (p * part_ref.shape[0] + y) * cols
            out_ref[:, at : at + cols] = total[:, p * cols : (p + 1) * cols]


def gather(part):
    vmem = pl.BlockSpec(memory_space=pltpu.VMEM)
    return pl.pallas_call(
        gather_kernel,
        out_shape=jax.ShapeDtypeStruct((part.shape[2], part.shape[0] * part.shape[3]), jnp.bfloat16),
        in_specs=[vmem],
        out_specs=vmem,
        compiler_params=pltpu.CompilerParams(vmem_limit_bytes=16 * 1024 * 1024),
        name="gather",
    )(part)


def per_device(values, gate, spectrum, bias, out_weight):
    rows, group = values.shape
    width = group // (Z * Y)
    cols = out_weight.shape[1]
    weight = lax.all_gather(out_weight, "z", axis=0, tiled=False)

    def by_y(array):
        return array.T.reshape(Z, Y, width, rows).transpose(1, 0, 2, 3).reshape(Y, Z, width * rows)

    near = jnp.concatenate([by_y(values), by_y(gate)], axis=1)
    near = lax.all_to_all(near, "y", split_axis=0, concat_axis=0, tiled=True)
    sig, gat = near[:, :Z], near[:, Z:]
    moved = lax.all_to_all(sig.transpose(1, 0, 2), "z", split_axis=0, concat_axis=0, tiled=True)
    conv = long_conv(moved.reshape(Z * Y, width * rows), spectrum.reshape(width, TALL, TALL))
    conv = lax.all_to_all(conv.reshape(Z, Y, width * rows), "z", split_axis=0, concat_axis=0, tiled=True)
    skip = lax.dynamic_index_in_dim(bias.reshape(Z, Y, width), lax.axis_index("y"), 1, keepdims=False)
    skip = jnp.broadcast_to(skip[:, :, None], (Z, width, rows)).reshape(Z, width * rows)
    conv = conv.transpose(1, 0, 2).astype(jnp.float32)
    gated = (gat.astype(jnp.float32) * (conv + skip[None] * sig.astype(jnp.float32))).astype(jnp.bfloat16)

    left = gated.reshape(Y, Z, width, rows).transpose(1, 2, 0, 3).reshape(Z, width, Y * rows)
    wide = jnp.broadcast_to(left[None], (Y,) + left.shape)
    wide = lax.all_to_all(wide, "y", split_axis=0, concat_axis=0, tiled=True)

    me = lax.axis_index("core").astype(jnp.int32).reshape(1)
    left = turn(wide)
    send = project(1 - me, left, weight, "project_send")
    other = lax.ppermute(send, "core", [(0, 1), (1, 0)])
    keep = project(me, left, weight, "project_keep")
    part = (keep.astype(jnp.float32) + other.astype(jnp.float32)).astype(jnp.bfloat16)
    part = part.reshape((Y * X,) + part.shape[2:])
    part = lax.all_to_all(part, ("y", "x"), split_axis=0, concat_axis=0, tiled=True)
    return gather(part.reshape(Y, X, rows, -1))


def solution(mesh):
    names = ("z", "y", "x", "core")
    fine = Mesh(mesh.devices.reshape(Z, Y, X, CORE), names)
    seq, chan = names[:2], names[2:]
    placed = (
        P(seq, chan),
        P(seq, chan),
        P(chan + seq, None, None),
        P(chan),
        P(chan, seq),
    )
    return jax.shard_map(
        per_device, mesh=fine, in_specs=placed, out_specs=P(seq, chan), check_vma=False
    )
```

```python
import jax
import jax.numpy as jnp
import numpy as np
from jax import lax
from jax.experimental import pallas as pl
from jax.experimental.pallas import tpu as pltpu
from jax.sharding import Mesh, PartitionSpec as P

ZH, ZL, Y, X, CORE = 8, 2, 4, 4, 2
NEAR = ZL * Y
HALF = 64
TALL = 128
FFT = 8192


def split(table):
    top = table.astype(jnp.bfloat16)
    rest = (table - top.astype(np.float64)).astype(jnp.bfloat16)
    return top, rest


def fft_tables():
    turn = 2.0 * np.pi
    k, s, m = np.arange(TALL), np.arange(HALF), np.arange(HALF)
    one = turn * (np.outer(k, s) % TALL) / TALL
    first = np.concatenate([np.cos(one), np.sin(one)], 0)
    first = np.concatenate(split(first), 1)
    spin = turn * np.outer(k, m) / FFT
    cos, sin = np.cos(spin), np.sin(spin)
    fwd = np.stack([np.concatenate([cos, -sin], 1), np.concatenate([-sin, -cos], 1)])
    inv = np.stack([np.concatenate([cos, cos], 1), np.concatenate([-sin, sin], 1)])
    two = turn * (np.outer(m, m) % HALF) / HALF
    c2, s2 = np.cos(two), np.sin(two)
    ahead = np.block([[c2, -s2, -s2, c2], [s2, c2, c2, s2]])
    back = np.block([[c2, s2, s2, c2], [-s2, c2, c2, -s2]])

    def triple(table):
        top, rest = split(table)
        return np.concatenate([top, top, rest], 0)

    four = turn * (np.outer(s, k) % TALL) / TALL
    last = np.concatenate([np.cos(four), -np.sin(four)], 0) / FFT
    top, rest = split(last)
    last = np.concatenate([top, top, rest], 1)
    return (
        first,
        np.concatenate([fwd, inv]).astype(np.float32),
        np.stack([triple(ahead), triple(back)]),
        last,
    )


def pieces(value):
    top = value.astype(jnp.bfloat16)
    rest = (value - top.astype(jnp.float32)).astype(jnp.bfloat16)
    return [top, rest, top]


GANG = 4


def conv_kernel(both_ref, spec_ref, skip_ref, first_ref, spin_ref, mid_ref, last_ref, out_ref):
    width = 2 * HALF
    left = lax.broadcasted_iota(jnp.int32, (1, width), 1) < HALF
    fp, fq, ip, iq = [spin_ref[i] for i in range(4)]

    def swap(value):
        return pltpu.roll(value, HALF, 1)

    def dot(one, two):
        return jnp.dot(one, two, preferred_element_type=jnp.float32)

    for start in range(0, both_ref.shape[0], GANG):
        gang = range(GANG)
        data = [both_ref[start + c].astype(jnp.float32) for c in gang]
        other = [swap(data[c]) for c in gang]
        wide = jnp.concatenate([jnp.where(left, data[c], other[c]) for c in gang], 1).astype(jnp.bfloat16)
        both = dot(first_ref[...], jnp.concatenate([wide, wide], 0))
        at = [slice(c * width, (c + 1) * width) for c in gang]
        tall = [slice(c * TALL, (c + 1) * TALL) for c in gang]
        turned = jnp.concatenate([both[:TALL, at[c]] * fp + both[TALL:, at[c]] * fq for c in gang], 0)
        freq = dot(jnp.concatenate(pieces(turned), 1), mid_ref[0])
        filt = jnp.concatenate([spec_ref[start + c].T for c in gang], 0)
        turned_filt = swap(filt)
        prod = freq[:, :width] * jnp.where(left, filt, turned_filt) + freq[:, width:] * jnp.where(
            left, -turned_filt, filt
        )
        back = dot(jnp.concatenate(pieces(prod), 1), mid_ref[1])
        spun = jnp.concatenate([back[tall[c], :width] * ip + back[tall[c], width:] * iq for c in gang], 1)
        ends = dot(last_ref[...], jnp.concatenate(pieces(spun), 0))
        for c in range(0, GANG, 2):
            even, odd = ends[:, at[c]], ends[:, at[c + 1]]
            conv = jnp.where(left, even[:HALF], odd[HALF:]) + swap(jnp.where(left, odd[:HALF], even[HALF:]))
            conv = conv.astype(jnp.bfloat16).astype(jnp.float32)
            value = jnp.where(left, data[c], other[c + 1])
            gate = jnp.where(left, other[c], data[c + 1])
            lanes = slice((start + c) * HALF, (start + c + 2) * HALF)
            out_ref[:, lanes] = (gate * (conv + skip_ref[:, lanes] * value)).astype(jnp.bfloat16)


def gated_conv(both, spec, skip):
    width, length, lanes = both.shape
    tables = fft_tables()
    vmem = pl.BlockSpec(memory_space=pltpu.VMEM)
    return pl.pallas_call(
        conv_kernel,
        out_shape=jax.ShapeDtypeStruct((length, width * lanes // 2), jnp.bfloat16),
        in_specs=[vmem] * 7,
        out_specs=vmem,
        compiler_params=pltpu.CompilerParams(vmem_limit_bytes=32 * 1024 * 1024),
        cost_estimate=pl.CostEstimate(flops=1_200_000_000, bytes_accessed=2_000_000, transcendentals=0),
        name="gated_conv",
    )(both, spec, skip, *[jnp.asarray(t) for t in tables])


def spread_kernel(left_ref, out_ref):
    for spot in range(out_ref.shape[0]):
        out_ref[spot] = left_ref[...]


def spread(left):
    vmem = pl.BlockSpec(memory_space=pltpu.VMEM)
    return pl.pallas_call(
        spread_kernel,
        out_shape=jax.ShapeDtypeStruct((NEAR,) + left.shape, jnp.bfloat16),
        in_specs=[vmem],
        out_specs=vmem,
        compiler_params=pltpu.CompilerParams(vmem_limit_bytes=32 * 1024 * 1024),
        name="spread",
    )(left)


def turn_kernel(left_ref, out_ref):
    near, far = left_ref.shape[:2]
    blocks = [left_ref[a, b] for b in range(far) for a in range(near)]
    out_ref[...] = jnp.concatenate(blocks, 0).T


def turn(left):
    near, far, width, tokens = left.shape
    vmem = pl.BlockSpec(memory_space=pltpu.VMEM)
    return pl.pallas_call(
        turn_kernel,
        out_shape=jax.ShapeDtypeStruct((tokens, near * far * width), jnp.bfloat16),
        in_specs=[vmem],
        out_specs=vmem,
        compiler_params=pltpu.CompilerParams(vmem_limit_bytes=32 * 1024 * 1024),
        name="turn",
    )(left)


def project_kernel(me_ref, left_ref, weight_ref, keep_ref, send_ref, held_ref, sems):
    blocks, _, cols = held_ref.shape
    copies = [pltpu.make_async_copy(weight_ref.at[i], held_ref.at[i], sems.at[i]) for i in range(blocks)]
    for copy in copies:
        copy.start()
    left = left_ref[...]
    mine = me_ref[0]
    for x in range(0, X, 2):
        for i in range(x * CORE, (x + 2) * CORE):
            copies[i].wait()
        order = [(x + k) * CORE + core for core in (mine, 1 - mine) for k in range(2)]
        weight = jnp.concatenate([held_ref[i] for i in order], 1)
        part = jnp.dot(left, weight, preferred_element_type=jnp.float32).astype(jnp.bfloat16)
        for k in range(2):
            for to_ref, at in ((keep_ref, k), (send_ref, 2 + k)):
                to_ref[:, x + k] = part[:, at * cols : (at + 1) * cols].reshape(to_ref.shape[0], HALF, cols)


def project(me, left, weight):
    tokens, depth = left.shape
    blocks, _, cols = weight.shape
    vmem = pl.BlockSpec(memory_space=pltpu.VMEM)
    return pl.pallas_call(
        project_kernel,
        out_shape=[jax.ShapeDtypeStruct((tokens // HALF, X, HALF, cols), jnp.bfloat16)] * 2,
        in_specs=[pl.BlockSpec(memory_space=pltpu.SMEM), vmem, pl.BlockSpec(memory_space=pl.ANY)],
        out_specs=[vmem, vmem],
        scratch_shapes=[pltpu.VMEM(weight.shape, weight.dtype), pltpu.SemaphoreType.DMA((blocks,))],
        compiler_params=pltpu.CompilerParams(vmem_limit_bytes=52 * 1024 * 1024),
        cost_estimate=pl.CostEstimate(flops=2 * depth * tokens * blocks * cols, bytes_accessed=4_000_000, transcendentals=0),
        name="project",
    )(me, left, weight)


def pair_kernel(values_ref, gate_ref, out_ref, held_ref, sems):
    copies = [pltpu.make_async_copy(ref, held_ref.at[i], sems.at[i]) for i, ref in enumerate((values_ref, gate_ref))]
    for copy in copies:
        copy.start()
    for copy in copies:
        copy.wait()
    out_ref[...] = jnp.concatenate([held_ref[0], held_ref[1]], 0).T


def pair(values, gate):
    rows, group = values.shape
    away = pl.BlockSpec(memory_space=pl.ANY)
    return pl.pallas_call(
        pair_kernel,
        out_shape=jax.ShapeDtypeStruct((group, 2 * rows), jnp.bfloat16),
        in_specs=[away, away],
        out_specs=pl.BlockSpec(memory_space=pltpu.VMEM),
        scratch_shapes=[pltpu.VMEM((2, rows, group), jnp.bfloat16), pltpu.SemaphoreType.DMA((2,))],
        compiler_params=pltpu.CompilerParams(vmem_limit_bytes=56 * 1024 * 1024),
        name="pair",
    )(values, gate)


def per_device(values, gate, spectrum, bias, out_weight):
    rows, group = values.shape
    width = group // (ZH * NEAR)
    cols = out_weight.shape[1]
    weight = lax.all_gather(out_weight, "zh", axis=0, tiled=False)

    nseq = ZH * NEAR
    both = pair(values, gate).reshape(nseq, width, 2 * rows)
    both = lax.all_to_all(both, ("zh", "zl", "y"), split_axis=0, concat_axis=0, tiled=True)
    seq = lax.axis_index(("zh", "zl", "y"))
    skip = lax.dynamic_slice(bias, (seq * width,), (width,))
    skip = jnp.broadcast_to(skip[:, None], (width, rows)).reshape(1, width * rows)
    gated = gated_conv(both.transpose(1, 0, 2), spectrum.reshape(width, TALL, TALL), skip)

    gated = gated.reshape(ZH, NEAR, width * rows)
    gated = lax.all_to_all(gated, "zh", split_axis=0, concat_axis=0, tiled=True)
    left = gated.reshape(ZH, NEAR, width, rows).transpose(0, 2, 1, 3).reshape(ZH, width, NEAR * rows)

    def there(block):
        wide = jnp.broadcast_to(block[None], (NEAR,) + block.shape)
        return turn(lax.all_to_all(wide, ("zl", "y"), split_axis=0, concat_axis=0, tiled=True))

    def again(block):
        wide = lax.all_to_all(spread(block), ("zl", "y"), split_axis=0, concat_axis=0, tiled=True)
        return wide.transpose(3, 1, 0, 2).reshape(NEAR * rows, group)

    left = lax.cond(bias[0] < 1e9, there, again, left)
    me = lax.axis_index("core").astype(jnp.int32).reshape(1)
    keep, send = project(me, left, weight)
    other = lax.ppermute(send, "core", [(0, 1), (1, 0)])
    part = (keep.astype(jnp.float32) + other.astype(jnp.float32)).astype(jnp.bfloat16)
    part = part.reshape((NEAR * X,) + part.shape[2:])
    part = lax.all_to_all(part, ("zl", "y", "x"), split_axis=0, concat_axis=0, tiled=True)
    total = jnp.sum(part.reshape(NEAR, X, rows, cols).astype(jnp.float32), axis=1).astype(jnp.bfloat16)
    return total.transpose(1, 0, 2).reshape(rows, -1)


def solution(mesh):
    names = ("zh", "zl", "y", "x", "core")
    fine = Mesh(mesh.devices.reshape(ZH, ZL, Y, X, CORE), names)
    seq, chan = names[:3], names[3:]
    placed = (
        P(seq, chan),
        P(seq, chan),
        P(chan + seq, None, None),
        P(chan),
        P(chan, seq),
    )
    return jax.shard_map(
        per_device, mesh=fine, in_specs=placed, out_specs=P(seq, chan), check_vma=False
    )
```

```python
import jax
import jax.numpy as jnp
import numpy as np
from jax import lax
from jax.experimental import pallas as pl
from jax.experimental.pallas import tpu as pltpu
from jax.sharding import Mesh, PartitionSpec as P

ZH, ZL, Y, X, CORE = 8, 2, 4, 4, 2
NEAR = ZL * Y
HALF = 64
TALL = 128
FFT = 8192


def split(table):
    top = table.astype(jnp.bfloat16)
    rest = (table - top.astype(np.float64)).astype(jnp.bfloat16)
    return top, rest


def fft_tables():
    turn = 2.0 * np.pi
    k, s, m = np.arange(TALL), np.arange(HALF), np.arange(HALF)
    one = turn * (np.outer(k, s) % TALL) / TALL
    first = np.concatenate([np.cos(one), np.sin(one)], 0)
    first = np.concatenate(split(first), 1)
    spin = turn * np.outer(k, m) / FFT
    cos, sin = np.cos(spin), np.sin(spin)
    fwd = np.stack([np.concatenate([cos, -sin], 1), np.concatenate([-sin, -cos], 1)])
    inv = np.stack([np.concatenate([cos, cos], 1), np.concatenate([-sin, sin], 1)])
    two = turn * (np.outer(m, m) % HALF) / HALF
    c2, s2 = np.cos(two), np.sin(two)
    ahead = np.block([[c2, -s2, -s2, c2], [s2, c2, c2, s2]])
    back = np.block([[c2, s2, s2, c2], [-s2, c2, c2, -s2]])

    def triple(table):
        top, rest = split(table)
        return np.concatenate([top, top, rest], 0)

    four = turn * (np.outer(s, k) % TALL) / TALL
    last = np.concatenate([np.cos(four), -np.sin(four)], 0) / FFT
    top, rest = split(last)
    last = np.concatenate([top, top, rest], 1)
    return (
        first,
        np.concatenate([fwd, inv]).astype(np.float32),
        np.stack([triple(ahead), triple(back)]),
        last,
    )


def pieces(value):
    top = value.astype(jnp.bfloat16)
    rest = (value - top.astype(jnp.float32)).astype(jnp.bfloat16)
    return [top, rest, top]


GANG = 8


def conv_kernel(both_ref, spec_ref, skip_ref, first_ref, spin_ref, mid_ref, last_ref, out_ref):
    width = 2 * HALF
    left = lax.broadcasted_iota(jnp.int32, (1, width), 1) < HALF
    fp, fq, ip, iq = [spin_ref[i] for i in range(4)]

    def swap(value):
        return pltpu.roll(value, HALF, 1)

    def dot(one, two):
        return jnp.dot(one, two, preferred_element_type=jnp.float32)

    for start in range(0, both_ref.shape[0], GANG):
        gang = range(GANG)
        data = [both_ref[start + c].astype(jnp.float32) for c in gang]
        other = [swap(data[c]) for c in gang]
        wide = jnp.concatenate([jnp.where(left, data[c], other[c]) for c in gang], 1).astype(jnp.bfloat16)
        both = dot(first_ref[...], jnp.concatenate([wide, wide], 0))
        at = [slice(c * width, (c + 1) * width) for c in gang]
        tall = [slice(c * TALL, (c + 1) * TALL) for c in gang]
        turned = jnp.concatenate([both[:TALL, at[c]] * fp + both[TALL:, at[c]] * fq for c in gang], 0)
        freq = dot(jnp.concatenate(pieces(turned), 1), mid_ref[0])
        filt = jnp.concatenate([spec_ref[start + c].T for c in gang], 0)
        turned_filt = swap(filt)
        prod = freq[:, :width] * jnp.where(left, filt, turned_filt) + freq[:, width:] * jnp.where(
            left, -turned_filt, filt
        )
        back = dot(jnp.concatenate(pieces(prod), 1), mid_ref[1])
        spun = jnp.concatenate([back[tall[c], :width] * ip + back[tall[c], width:] * iq for c in gang], 1)
        ends = dot(last_ref[...], jnp.concatenate(pieces(spun), 0))
        for c in range(0, GANG, 2):
            even, odd = ends[:, at[c]], ends[:, at[c + 1]]
            conv = jnp.where(left, even[:HALF], odd[HALF:]) + swap(jnp.where(left, odd[:HALF], even[HALF:]))
            conv = conv.astype(jnp.bfloat16).astype(jnp.float32)
            value = jnp.where(left, data[c], other[c + 1])
            gate = jnp.where(left, other[c], data[c + 1])
            lanes = slice((start + c) * HALF, (start + c + 2) * HALF)
            out_ref[:, lanes] = (gate * (conv + skip_ref[:, lanes] * value)).astype(jnp.bfloat16)


def gated_conv(both, spec, skip):
    width, length, lanes = both.shape
    tables = fft_tables()
    vmem = pl.BlockSpec(memory_space=pltpu.VMEM)
    return pl.pallas_call(
        conv_kernel,
        out_shape=jax.ShapeDtypeStruct((length, width * lanes // 2), jnp.bfloat16),
        in_specs=[vmem] * 7,
        out_specs=vmem,
        compiler_params=pltpu.CompilerParams(vmem_limit_bytes=32 * 1024 * 1024),
        cost_estimate=pl.CostEstimate(flops=1_200_000_000, bytes_accessed=2_000_000, transcendentals=0),
        name="gated_conv",
    )(both, spec, skip, *[jnp.asarray(t) for t in tables])


def spread_kernel(left_ref, out_ref):
    for spot in range(out_ref.shape[0]):
        out_ref[spot] = left_ref[...]


def spread(left):
    vmem = pl.BlockSpec(memory_space=pltpu.VMEM)
    return pl.pallas_call(
        spread_kernel,
        out_shape=jax.ShapeDtypeStruct((NEAR,) + left.shape, jnp.bfloat16),
        in_specs=[vmem],
        out_specs=vmem,
        compiler_params=pltpu.CompilerParams(vmem_limit_bytes=32 * 1024 * 1024),
        name="spread",
    )(left)


def turn_kernel(left_ref, out_ref):
    near, far = left_ref.shape[:2]
    blocks = [left_ref[a, b] for b in range(far) for a in range(near)]
    out_ref[...] = jnp.concatenate(blocks, 0).T


def turn(left):
    near, far, width, tokens = left.shape
    vmem = pl.BlockSpec(memory_space=pltpu.VMEM)
    return pl.pallas_call(
        turn_kernel,
        out_shape=jax.ShapeDtypeStruct((tokens, near * far * width), jnp.bfloat16),
        in_specs=[vmem],
        out_specs=vmem,
        compiler_params=pltpu.CompilerParams(vmem_limit_bytes=32 * 1024 * 1024),
        name="turn",
    )(left)


def project_kernel(side_ref, left_ref, weight_ref, out_ref, held_ref, sems):
    blocks, _, cols = held_ref.shape
    copies = [
        pltpu.make_async_copy(weight_ref.at[x * CORE + side_ref[0]], held_ref.at[x], sems.at[x]) for x in range(blocks)
    ]
    for copy in copies:
        copy.start()
    for copy in copies:
        copy.wait()
    weight = jnp.concatenate([held_ref[x] for x in range(blocks)], 1)
    part = jnp.dot(left_ref[...], weight, preferred_element_type=jnp.float32).astype(jnp.bfloat16)
    for x in range(blocks):
        out_ref[:, x] = part[:, x * cols : (x + 1) * cols].reshape(out_ref.shape[0], HALF, cols)


def project(side, left, weight, name):
    tokens, depth = left.shape
    blocks, _, cols = weight.shape
    half = blocks // CORE
    vmem = pl.BlockSpec(memory_space=pltpu.VMEM)
    return pl.pallas_call(
        project_kernel,
        out_shape=jax.ShapeDtypeStruct((tokens // HALF, X, HALF, cols), jnp.bfloat16),
        in_specs=[pl.BlockSpec(memory_space=pltpu.SMEM), vmem, pl.BlockSpec(memory_space=pl.ANY)],
        out_specs=vmem,
        scratch_shapes=[pltpu.VMEM((half, depth, cols), weight.dtype), pltpu.SemaphoreType.DMA((half,))],
        compiler_params=pltpu.CompilerParams(vmem_limit_bytes=52 * 1024 * 1024),
        cost_estimate=pl.CostEstimate(flops=2 * depth * tokens * half * cols, bytes_accessed=3_000_000, transcendentals=0),
        name=name,
    )(side, left, weight)


def pair_kernel(values_ref, gate_ref, out_ref, held_ref, sems):
    copies = [pltpu.make_async_copy(ref, held_ref.at[i], sems.at[i]) for i, ref in enumerate((values_ref, gate_ref))]
    for copy in copies:
        copy.start()
    for copy in copies:
        copy.wait()
    out_ref[...] = jnp.concatenate([held_ref[0], held_ref[1]], 0).T


def pair(values, gate):
    rows, group = values.shape
    away = pl.BlockSpec(memory_space=pl.ANY)
    return pl.pallas_call(
        pair_kernel,
        out_shape=jax.ShapeDtypeStruct((group, 2 * rows), jnp.bfloat16),
        in_specs=[away, away],
        out_specs=pl.BlockSpec(memory_space=pltpu.VMEM),
        scratch_shapes=[pltpu.VMEM((2, rows, group), jnp.bfloat16), pltpu.SemaphoreType.DMA((2,))],
        compiler_params=pltpu.CompilerParams(vmem_limit_bytes=56 * 1024 * 1024),
        name="pair",
    )(values, gate)


def per_device(values, gate, spectrum, bias, out_weight):
    rows, group = values.shape
    width = group // (ZH * NEAR)
    cols = out_weight.shape[1]
    weight = lax.all_gather(out_weight, "zh", axis=0, tiled=False)

    nseq = ZH * NEAR
    both = pair(values, gate).reshape(nseq, width, 2 * rows)
    both = lax.all_to_all(both, ("zh", "zl", "y"), split_axis=0, concat_axis=0, tiled=True)
    seq = lax.axis_index(("zh", "zl", "y"))
    skip = lax.dynamic_slice(bias, (seq * width,), (width,))
    skip = jnp.broadcast_to(skip[:, None], (width, rows)).reshape(1, width * rows)
    gated = gated_conv(both.transpose(1, 0, 2), spectrum.reshape(width, TALL, TALL), skip)

    gated = gated.reshape(ZH, NEAR, width * rows)
    gated = lax.all_to_all(gated, "zh", split_axis=0, concat_axis=0, tiled=True)
    left = gated.reshape(ZH, NEAR, width, rows).transpose(0, 2, 1, 3).reshape(ZH, width, NEAR * rows)

    def there(block):
        wide = jnp.broadcast_to(block[None], (NEAR,) + block.shape)
        return turn(lax.all_to_all(wide, ("zl", "y"), split_axis=0, concat_axis=0, tiled=True))

    def again(block):
        wide = lax.all_to_all(spread(block), ("zl", "y"), split_axis=0, concat_axis=0, tiled=True)
        return wide.transpose(3, 1, 0, 2).reshape(NEAR * rows, group)

    left = lax.cond(bias[0] < 1e9, there, again, left)
    me = lax.axis_index("core").astype(jnp.int32).reshape(1)
    send = project(1 - me, left, weight, "project_send")
    other = lax.ppermute(send, "core", [(0, 1), (1, 0)])
    keep = project(me, left, weight, "project_keep")
    part = (keep.astype(jnp.float32) + other.astype(jnp.float32)).astype(jnp.bfloat16)
    part = part.reshape((NEAR * X,) + part.shape[2:])
    part = lax.all_to_all(part, ("zl", "y", "x"), split_axis=0, concat_axis=0, tiled=True)
    total = jnp.sum(part.reshape(NEAR, X, rows, cols).astype(jnp.float32), axis=1).astype(jnp.bfloat16)
    return total.transpose(1, 0, 2).reshape(rows, -1)


def solution(mesh):
    names = ("zh", "zl", "y", "x", "core")
    fine = Mesh(mesh.devices.reshape(ZH, ZL, Y, X, CORE), names)
    seq, chan = names[:3], names[3:]
    placed = (
        P(seq, chan),
        P(seq, chan),
        P(chan + seq, None, None),
        P(chan),
        P(chan, seq),
    )
    return jax.shard_map(
        per_device, mesh=fine, in_specs=placed, out_specs=P(seq, chan), check_vma=False
    )
```

```python
import jax
import jax.numpy as jnp
import numpy as np
from jax import lax
from jax.experimental import pallas as pl
from jax.experimental.pallas import tpu as pltpu
from jax.sharding import Mesh, PartitionSpec as P

ZH, ZL, Y, X, CORE = 8, 2, 4, 4, 2
NEAR = ZL * Y
HALF = 64
TALL = 128
FFT = 8192


def split(table):
    top = table.astype(jnp.bfloat16)
    rest = (table - top.astype(np.float64)).astype(jnp.bfloat16)
    return top, rest


def fft_tables():
    turn = 2.0 * np.pi
    k, s, m = np.arange(TALL), np.arange(HALF), np.arange(HALF)
    one = turn * (np.outer(k, s) % TALL) / TALL
    first = np.concatenate([np.cos(one), np.sin(one)], 0)
    first = np.concatenate(split(first), 1)
    spin = turn * np.outer(k, m) / FFT
    cos, sin = np.cos(spin), np.sin(spin)
    fwd = np.stack([np.concatenate([cos, -sin], 1), np.concatenate([-sin, -cos], 1)])
    inv = np.stack([np.concatenate([cos, cos], 1), np.concatenate([-sin, sin], 1)])
    two = turn * (np.outer(m, m) % HALF) / HALF
    c2, s2 = np.cos(two), np.sin(two)
    ahead = np.block([[c2, -s2, -s2, c2], [s2, c2, c2, s2]])
    back = np.block([[c2, s2, s2, c2], [-s2, c2, c2, -s2]])

    def triple(table):
        top, rest = split(table)
        return np.concatenate([top, top, rest], 0)

    four = turn * (np.outer(s, k) % TALL) / TALL
    last = np.concatenate([np.cos(four), -np.sin(four)], 0) / FFT
    top, rest = split(last)
    last = np.concatenate([top, top, rest], 1)
    return (
        first,
        np.concatenate([fwd, inv]).astype(np.float32),
        np.stack([triple(ahead), triple(back)]),
        last,
    )


def pieces(value):
    top = value.astype(jnp.bfloat16)
    rest = (value - top.astype(jnp.float32)).astype(jnp.bfloat16)
    return [top, rest, top]


GANG = 16


def conv_kernel(both_ref, spec_ref, skip_ref, first_ref, spin_ref, mid_ref, last_ref, out_ref):
    width = 2 * HALF
    left = lax.broadcasted_iota(jnp.int32, (1, width), 1) < HALF
    fp, fq, ip, iq = [spin_ref[i] for i in range(4)]

    def swap(value):
        return pltpu.roll(value, HALF, 1)

    def dot(one, two):
        return jnp.dot(one, two, preferred_element_type=jnp.float32)

    for start in range(0, both_ref.shape[0], GANG):
        gang = range(GANG)
        data = [both_ref[start + c].astype(jnp.float32) for c in gang]
        other = [swap(data[c]) for c in gang]
        wide = jnp.concatenate([jnp.where(left, data[c], other[c]) for c in gang], 1).astype(jnp.bfloat16)
        both = dot(first_ref[...], jnp.concatenate([wide, wide], 0))
        at = [slice(c * width, (c + 1) * width) for c in gang]
        tall = [slice(c * TALL, (c + 1) * TALL) for c in gang]
        turned = jnp.concatenate([both[:TALL, at[c]] * fp + both[TALL:, at[c]] * fq for c in gang], 0)
        freq = dot(jnp.concatenate(pieces(turned), 1), mid_ref[0])
        filt = jnp.concatenate([spec_ref[start + c].T for c in gang], 0)
        turned_filt = swap(filt)
        prod = freq[:, :width] * jnp.where(left, filt, turned_filt) + freq[:, width:] * jnp.where(
            left, -turned_filt, filt
        )
        back = dot(jnp.concatenate(pieces(prod), 1), mid_ref[1])
        spun = jnp.concatenate([back[tall[c], :width] * ip + back[tall[c], width:] * iq for c in gang], 1)
        ends = dot(last_ref[...], jnp.concatenate(pieces(spun), 0))
        for c in range(0, GANG, 2):
            even, odd = ends[:, at[c]], ends[:, at[c + 1]]
            conv = jnp.where(left, even[:HALF], odd[HALF:]) + swap(jnp.where(left, odd[:HALF], even[HALF:]))
            conv = conv.astype(jnp.bfloat16).astype(jnp.float32)
            value = jnp.where(left, data[c], other[c + 1])
            gate = jnp.where(left, other[c], data[c + 1])
            lanes = slice((start + c) * HALF, (start + c + 2) * HALF)
            out_ref[:, lanes] = (gate * (conv + skip_ref[:, lanes] * value)).astype(jnp.bfloat16)


def gated_conv(both, spec, skip):
    width, length, lanes = both.shape
    tables = fft_tables()
    vmem = pl.BlockSpec(memory_space=pltpu.VMEM)
    return pl.pallas_call(
        conv_kernel,
        out_shape=jax.ShapeDtypeStruct((length, width * lanes // 2), jnp.bfloat16),
        in_specs=[vmem] * 7,
        out_specs=vmem,
        compiler_params=pltpu.CompilerParams(vmem_limit_bytes=32 * 1024 * 1024),
        cost_estimate=pl.CostEstimate(flops=1_200_000_000, bytes_accessed=2_000_000, transcendentals=0),
        name="gated_conv",
    )(both, spec, skip, *[jnp.asarray(t) for t in tables])


def spread_kernel(left_ref, out_ref):
    for spot in range(out_ref.shape[0]):
        out_ref[spot] = left_ref[...]


def spread(left):
    vmem = pl.BlockSpec(memory_space=pltpu.VMEM)
    return pl.pallas_call(
        spread_kernel,
        out_shape=jax.ShapeDtypeStruct((NEAR,) + left.shape, jnp.bfloat16),
        in_specs=[vmem],
        out_specs=vmem,
        compiler_params=pltpu.CompilerParams(vmem_limit_bytes=32 * 1024 * 1024),
        name="spread",
    )(left)


def turn_kernel(left_ref, out_ref):
    near, far = left_ref.shape[:2]
    blocks = [left_ref[a, b] for b in range(far) for a in range(near)]
    out_ref[...] = jnp.concatenate(blocks, 0).T


def turn(left):
    near, far, width, tokens = left.shape
    vmem = pl.BlockSpec(memory_space=pltpu.VMEM)
    return pl.pallas_call(
        turn_kernel,
        out_shape=jax.ShapeDtypeStruct((tokens, near * far * width), jnp.bfloat16),
        in_specs=[vmem],
        out_specs=vmem,
        compiler_params=pltpu.CompilerParams(vmem_limit_bytes=32 * 1024 * 1024),
        name="turn",
    )(left)


def project_kernel(side_ref, left_ref, weight_ref, out_ref, held_ref, sems):
    blocks, _, cols = held_ref.shape
    copies = [
        pltpu.make_async_copy(weight_ref.at[x * CORE + side_ref[0]], held_ref.at[x], sems.at[x]) for x in range(blocks)
    ]
    for copy in copies:
        copy.start()
    for copy in copies:
        copy.wait()
    weight = jnp.concatenate([held_ref[x] for x in range(blocks)], 1)
    part = jnp.dot(left_ref[...], weight, preferred_element_type=jnp.float32).astype(jnp.bfloat16)
    for x in range(blocks):
        out_ref[:, x] = part[:, x * cols : (x + 1) * cols].reshape(out_ref.shape[0], HALF, cols)


def project(side, left, weight, name):
    tokens, depth = left.shape
    blocks, _, cols = weight.shape
    half = blocks // CORE
    vmem = pl.BlockSpec(memory_space=pltpu.VMEM)
    return pl.pallas_call(
        project_kernel,
        out_shape=jax.ShapeDtypeStruct((tokens // HALF, X, HALF, cols), jnp.bfloat16),
        in_specs=[pl.BlockSpec(memory_space=pltpu.SMEM), vmem, pl.BlockSpec(memory_space=pl.ANY)],
        out_specs=vmem,
        scratch_shapes=[pltpu.VMEM((half, depth, cols), weight.dtype), pltpu.SemaphoreType.DMA((half,))],
        compiler_params=pltpu.CompilerParams(vmem_limit_bytes=52 * 1024 * 1024),
        cost_estimate=pl.CostEstimate(flops=2 * depth * tokens * half * cols, bytes_accessed=3_000_000, transcendentals=0),
        name=name,
    )(side, left, weight)


def pair_kernel(values_ref, gate_ref, out_ref, held_ref, sems):
    copies = [pltpu.make_async_copy(ref, held_ref.at[i], sems.at[i]) for i, ref in enumerate((values_ref, gate_ref))]
    for copy in copies:
        copy.start()
    for copy in copies:
        copy.wait()
    out_ref[...] = jnp.concatenate([held_ref[0], held_ref[1]], 0).T


def pair(values, gate):
    rows, group = values.shape
    away = pl.BlockSpec(memory_space=pl.ANY)
    return pl.pallas_call(
        pair_kernel,
        out_shape=jax.ShapeDtypeStruct((group, 2 * rows), jnp.bfloat16),
        in_specs=[away, away],
        out_specs=pl.BlockSpec(memory_space=pltpu.VMEM),
        scratch_shapes=[pltpu.VMEM((2, rows, group), jnp.bfloat16), pltpu.SemaphoreType.DMA((2,))],
        compiler_params=pltpu.CompilerParams(vmem_limit_bytes=56 * 1024 * 1024),
        name="pair",
    )(values, gate)


def per_device(values, gate, spectrum, bias, out_weight):
    rows, group = values.shape
    width = group // (ZH * NEAR)
    cols = out_weight.shape[1]
    weight = lax.all_gather(out_weight, "zh", axis=0, tiled=False)

    nseq = ZH * NEAR
    both = pair(values, gate).reshape(nseq, width, 2 * rows)
    both = lax.all_to_all(both, ("zh", "zl", "y"), split_axis=0, concat_axis=0, tiled=True)
    seq = lax.axis_index(("zh", "zl", "y"))
    skip = lax.dynamic_slice(bias, (seq * width,), (width,))
    skip = jnp.broadcast_to(skip[:, None], (width, rows)).reshape(1, width * rows)
    gated = gated_conv(both.transpose(1, 0, 2), spectrum.reshape(width, TALL, TALL), skip)

    gated = gated.reshape(ZH, NEAR, width * rows)
    gated = lax.all_to_all(gated, "zh", split_axis=0, concat_axis=0, tiled=True)
    left = gated.reshape(ZH, NEAR, width, rows).transpose(0, 2, 1, 3).reshape(ZH, width, NEAR * rows)

    def there(block):
        wide = jnp.broadcast_to(block[None], (NEAR,) + block.shape)
        return turn(lax.all_to_all(wide, ("zl", "y"), split_axis=0, concat_axis=0, tiled=True))

    def again(block):
        wide = lax.all_to_all(spread(block), ("zl", "y"), split_axis=0, concat_axis=0, tiled=True)
        return wide.transpose(3, 1, 0, 2).reshape(NEAR * rows, group)

    left = lax.cond(bias[0] < 1e9, there, again, left)
    me = lax.axis_index("core").astype(jnp.int32).reshape(1)
    send = project(1 - me, left, weight, "project_send")
    other = lax.ppermute(send, "core", [(0, 1), (1, 0)])
    keep = project(me, left, weight, "project_keep")
    part = (keep.astype(jnp.float32) + other.astype(jnp.float32)).astype(jnp.bfloat16)
    part = part.reshape((NEAR * X,) + part.shape[2:])
    part = lax.all_to_all(part, ("zl", "y", "x"), split_axis=0, concat_axis=0, tiled=True)
    total = jnp.sum(part.reshape(NEAR, X, rows, cols).astype(jnp.float32), axis=1).astype(jnp.bfloat16)
    return total.transpose(1, 0, 2).reshape(rows, -1)


def solution(mesh):
    names = ("zh", "zl", "y", "x", "core")
    fine = Mesh(mesh.devices.reshape(ZH, ZL, Y, X, CORE), names)
    seq, chan = names[:3], names[3:]
    placed = (
        P(seq, chan),
        P(seq, chan),
        P(chan + seq, None, None),
        P(chan),
        P(chan, seq),
    )
    return jax.shard_map(
        per_device, mesh=fine, in_specs=placed, out_specs=P(seq, chan), check_vma=False
    )
```

```python
import jax
import jax.numpy as jnp
import numpy as np
from jax import lax
from jax.experimental import pallas as pl
from jax.experimental.pallas import tpu as pltpu
from jax.sharding import Mesh, PartitionSpec as P

ZH, ZL, Y, X, CORE = 8, 2, 4, 4, 2
NEAR = ZL * Y
HALF = 64
TALL = 128
FFT = 8192


def split(table):
    top = table.astype(jnp.bfloat16)
    rest = (table - top.astype(np.float64)).astype(jnp.bfloat16)
    return top, rest


def fft_tables():
    turn = 2.0 * np.pi
    k, s, m = np.arange(TALL), np.arange(HALF), np.arange(HALF)
    one = turn * (np.outer(k, s) % TALL) / TALL
    first = np.concatenate([np.cos(one), np.sin(one)], 0)
    first = np.concatenate(split(first), 1)
    spin = turn * np.outer(k, m) / FFT
    cos, sin = np.cos(spin), np.sin(spin)
    fwd = np.stack([np.concatenate([cos, -sin], 1), np.concatenate([-sin, -cos], 1)])
    inv = np.stack([np.concatenate([cos, cos], 1), np.concatenate([-sin, sin], 1)])
    two = turn * (np.outer(m, m) % HALF) / HALF
    c2, s2 = np.cos(two), np.sin(two)
    ahead = np.block([[c2, -s2, -s2, c2], [s2, c2, c2, s2]])
    back = np.block([[c2, s2, s2, c2], [-s2, c2, c2, -s2]])

    def triple(table):
        top, rest = split(table)
        return np.concatenate([top, top, rest], 0)

    four = turn * (np.outer(s, k) % TALL) / TALL
    last = np.concatenate([np.cos(four), -np.sin(four)], 0) / FFT
    top, rest = split(last)
    last = np.concatenate([top, top, rest], 1)
    return (
        first,
        np.concatenate([fwd, inv]).astype(np.float32),
        np.stack([triple(ahead), triple(back)]),
        last,
    )


def pieces(value):
    top = value.astype(jnp.bfloat16)
    rest = (value - top.astype(jnp.float32)).astype(jnp.bfloat16)
    return [top, rest, top]


GANG = 16


def conv_kernel(both_ref, spec_ref, skip_ref, first_ref, spin_ref, mid_ref, last_ref, out_ref):
    width = 2 * HALF
    left = lax.broadcasted_iota(jnp.int32, (1, width), 1) < HALF
    fp, fq, ip, iq = [spin_ref[i] for i in range(4)]

    def swap(value):
        return pltpu.roll(value, HALF, 1)

    def dot(one, two):
        return jnp.dot(one, two, preferred_element_type=jnp.float32)

    for start in range(0, both_ref.shape[0], GANG):
        gang = range(GANG)
        data = [both_ref[start + c].astype(jnp.float32) for c in gang]
        other = [swap(data[c]) for c in gang]
        wide = jnp.concatenate([jnp.where(left, data[c], other[c]) for c in gang], 1).astype(jnp.bfloat16)
        both = dot(first_ref[...], jnp.concatenate([wide, wide], 0))
        at = [slice(c * width, (c + 1) * width) for c in gang]
        tall = [slice(c * TALL, (c + 1) * TALL) for c in gang]
        turned = jnp.concatenate([both[:TALL, at[c]] * fp + both[TALL:, at[c]] * fq for c in gang], 0)
        freq = dot(jnp.concatenate(pieces(turned), 1), mid_ref[0])
        filt = jnp.concatenate([spec_ref[start + c].T for c in gang], 0)
        turned_filt = swap(filt)
        prod = freq[:, :width] * jnp.where(left, filt, turned_filt) + freq[:, width:] * jnp.where(
            left, -turned_filt, filt
        )
        back = dot(jnp.concatenate(pieces(prod), 1), mid_ref[1])
        spun = jnp.concatenate([back[tall[c], :width] * ip + back[tall[c], width:] * iq for c in gang], 1)
        ends = dot(last_ref[...], jnp.concatenate(pieces(spun), 0))
        for c in range(0, GANG, 2):
            even, odd = ends[:, at[c]], ends[:, at[c + 1]]
            conv = jnp.where(left, even[:HALF], odd[HALF:]) + swap(jnp.where(left, odd[:HALF], even[HALF:]))
            conv = conv.astype(jnp.bfloat16).astype(jnp.float32)
            value = jnp.where(left, data[c], other[c + 1])
            gate = jnp.where(left, other[c], data[c + 1])
            lanes = slice((start + c) * HALF, (start + c + 2) * HALF)
            out_ref[:, lanes] = (gate * (conv + skip_ref[:, lanes] * value)).astype(jnp.bfloat16)


def gated_conv(both, spec, skip):
    width, length, lanes = both.shape
    tables = fft_tables()
    vmem = pl.BlockSpec(memory_space=pltpu.VMEM)
    return pl.pallas_call(
        conv_kernel,
        out_shape=jax.ShapeDtypeStruct((length, width * lanes // 2), jnp.bfloat16),
        in_specs=[vmem] * 7,
        out_specs=vmem,
        compiler_params=pltpu.CompilerParams(vmem_limit_bytes=32 * 1024 * 1024),
        cost_estimate=pl.CostEstimate(flops=1_200_000_000, bytes_accessed=2_000_000, transcendentals=0),
        name="gated_conv",
    )(both, spec, skip, *[jnp.asarray(t) for t in tables])


def spread_kernel(left_ref, out_ref):
    for spot in range(out_ref.shape[0]):
        out_ref[spot] = left_ref[...]


def spread(left):
    vmem = pl.BlockSpec(memory_space=pltpu.VMEM)
    return pl.pallas_call(
        spread_kernel,
        out_shape=jax.ShapeDtypeStruct((NEAR,) + left.shape, jnp.bfloat16),
        in_specs=[vmem],
        out_specs=vmem,
        compiler_params=pltpu.CompilerParams(vmem_limit_bytes=32 * 1024 * 1024),
        name="spread",
    )(left)


def turn_kernel(left_ref, out_ref):
    near, far = left_ref.shape[:2]
    blocks = [left_ref[a, b] for b in range(far) for a in range(near)]
    out_ref[...] = jnp.concatenate(blocks, 0).T


def turn(left):
    near, far, width, tokens = left.shape
    vmem = pl.BlockSpec(memory_space=pltpu.VMEM)
    return pl.pallas_call(
        turn_kernel,
        out_shape=jax.ShapeDtypeStruct((tokens, near * far * width), jnp.bfloat16),
        in_specs=[vmem],
        out_specs=vmem,
        compiler_params=pltpu.CompilerParams(vmem_limit_bytes=32 * 1024 * 1024),
        name="turn",
    )(left)


def project_kernel(side_ref, left_ref, weight_ref, out_ref, held_ref, sems):
    blocks, _, cols = held_ref.shape
    copies = [
        pltpu.make_async_copy(weight_ref.at[x * CORE + side_ref[0]], held_ref.at[x], sems.at[x]) for x in range(blocks)
    ]
    for copy in copies:
        copy.start()
    for copy in copies:
        copy.wait()
    weight = jnp.concatenate([held_ref[x] for x in range(blocks)], 1)
    part = jnp.dot(left_ref[...], weight, preferred_element_type=jnp.float32).astype(jnp.bfloat16)
    for x in range(blocks):
        out_ref[:, x] = part[:, x * cols : (x + 1) * cols].reshape(out_ref.shape[0], HALF, cols)


def project(side, left, weight, name):
    tokens, depth = left.shape
    blocks, _, cols = weight.shape
    half = blocks // CORE
    vmem = pl.BlockSpec(memory_space=pltpu.VMEM)
    return pl.pallas_call(
        project_kernel,
        out_shape=jax.ShapeDtypeStruct((tokens // HALF, X, HALF, cols), jnp.bfloat16),
        in_specs=[pl.BlockSpec(memory_space=pltpu.SMEM), vmem, pl.BlockSpec(memory_space=pl.ANY)],
        out_specs=vmem,
        scratch_shapes=[pltpu.VMEM((half, depth, cols), weight.dtype), pltpu.SemaphoreType.DMA((half,))],
        compiler_params=pltpu.CompilerParams(vmem_limit_bytes=52 * 1024 * 1024),
        cost_estimate=pl.CostEstimate(flops=2 * depth * tokens * half * cols, bytes_accessed=3_000_000, transcendentals=0),
        name=name,
    )(side, left, weight)


PARTS = 2


def pair_kernel(values_ref, gate_ref, out_ref, held_ref, turned_ref, sems):
    wide = values_ref.shape[1] // PARTS
    at = [pl.ds(part * wide, wide) for part in range(PARTS)]
    arrive = [
        [
            pltpu.make_async_copy(ref.at[:, at[part]], held_ref.at[part, i], sems.at[part * 3 + i])
            for i, ref in enumerate((values_ref, gate_ref))
        ]
        for part in range(PARTS)
    ]
    leave = [
        pltpu.make_async_copy(turned_ref.at[part], out_ref.at[at[part]], sems.at[part * 3 + 2]) for part in range(PARTS)
    ]
    for copies in arrive:
        for copy in copies:
            copy.start()
    for part in range(PARTS):
        for copy in arrive[part]:
            copy.wait()
        turned_ref[part] = jnp.concatenate([held_ref[part, 0], held_ref[part, 1]], 0).T
        leave[part].start()
    for copy in leave:
        copy.wait()


def pair(values, gate):
    rows, group = values.shape
    away = pl.BlockSpec(memory_space=pl.ANY)
    return pl.pallas_call(
        pair_kernel,
        out_shape=jax.ShapeDtypeStruct((group, 2 * rows), jnp.bfloat16),
        in_specs=[away, away],
        out_specs=away,
        scratch_shapes=[
            pltpu.VMEM((PARTS, 2, rows, group // PARTS), jnp.bfloat16),
            pltpu.VMEM((PARTS, group // PARTS, 2 * rows), jnp.bfloat16),
            pltpu.SemaphoreType.DMA((3 * PARTS,)),
        ],
        compiler_params=pltpu.CompilerParams(vmem_limit_bytes=56 * 1024 * 1024),
        name="pair",
    )(values, gate)


def per_device(values, gate, spectrum, bias, out_weight):
    rows, group = values.shape
    width = group // (ZH * NEAR)
    cols = out_weight.shape[1]
    weight = lax.all_gather(out_weight, "zh", axis=0, tiled=False)

    nseq = ZH * NEAR
    both = pair(values, gate).reshape(nseq, width, 2 * rows)
    both = lax.all_to_all(both, ("zh", "zl", "y"), split_axis=0, concat_axis=0, tiled=True)
    seq = lax.axis_index(("zh", "zl", "y"))
    skip = lax.dynamic_slice(bias, (seq * width,), (width,))
    skip = jnp.broadcast_to(skip[:, None], (width, rows)).reshape(1, width * rows)
    gated = gated_conv(both.transpose(1, 0, 2), spectrum.reshape(width, TALL, TALL), skip)

    gated = gated.reshape(ZH, NEAR, width * rows)
    gated = lax.all_to_all(gated, "zh", split_axis=0, concat_axis=0, tiled=True)
    left = gated.reshape(ZH, NEAR, width, rows).transpose(0, 2, 1, 3).reshape(ZH, width, NEAR * rows)

    def there(block):
        wide = jnp.broadcast_to(block[None], (NEAR,) + block.shape)
        return turn(lax.all_to_all(wide, ("zl", "y"), split_axis=0, concat_axis=0, tiled=True))

    def again(block):
        wide = lax.all_to_all(spread(block), ("zl", "y"), split_axis=0, concat_axis=0, tiled=True)
        return wide.transpose(3, 1, 0, 2).reshape(NEAR * rows, group)

    left = lax.cond(bias[0] < 1e9, there, again, left)
    me = lax.axis_index("core").astype(jnp.int32).reshape(1)
    send = project(1 - me, left, weight, "project_send")
    other = lax.ppermute(send, "core", [(0, 1), (1, 0)])
    keep = project(me, left, weight, "project_keep")
    part = (keep.astype(jnp.float32) + other.astype(jnp.float32)).astype(jnp.bfloat16)
    part = part.reshape((NEAR * X,) + part.shape[2:])
    part = lax.all_to_all(part, ("zl", "y", "x"), split_axis=0, concat_axis=0, tiled=True)
    total = jnp.sum(part.reshape(NEAR, X, rows, cols).astype(jnp.float32), axis=1).astype(jnp.bfloat16)
    return total.transpose(1, 0, 2).reshape(rows, -1)


def solution(mesh):
    names = ("zh", "zl", "y", "x", "core")
    fine = Mesh(mesh.devices.reshape(ZH, ZL, Y, X, CORE), names)
    seq, chan = names[:3], names[3:]
    placed = (
        P(seq, chan),
        P(seq, chan),
        P(chan + seq, None, None),
        P(chan),
        P(chan, seq),
    )
    return jax.shard_map(
        per_device, mesh=fine, in_specs=placed, out_specs=P(seq, chan), check_vma=False
    )
```
